256 devices in a mesh: seq: 64 (over y, z, core), ch: 4 (over x).
Axes of the slice: x: 4, y: 4, z: 8, core: 2. Of those that a mesh axis runs over, the one named last changes fastest.
Arguments:
- gated_input: bfloat16 [262144, 1024], P('seq', 'ch'), may hold values from -6 to 6
- out_gate: bfloat16 [262144, 1024], P('seq', 'ch'), may hold values from -6 to 6
- grad_out: bfloat16 [262144, 1024], P('seq', 'ch'), may hold values from -6 to 6
- forward_inner: bfloat16 [512, 512], replicated, may hold values from -0.25 to 0.25
- forward_outer: bfloat16 [512, 512], replicated, may hold values from -0.25 to 0.25
- inverse_outer: bfloat16 [512, 512], replicated, may hold values from -0.25 to 0.25
- inverse_inner: bfloat16 [512, 512], replicated, may hold values from -0.25 to 0.25
- twiddle_forward: float32 [512, 512], P(None, 'seq'), may hold values from 0.5 to 1.5
- twiddle_inverse: float32 [512, 512], P(None, 'seq'), may hold values from 0.5 to 1.5
- filter_in: float32 [32, 128], replicated, may hold values from -1 to 1
- filter_bias: float32 [128], replicated, may hold values from -3.140625 to 3.140625
- filter_out: bfloat16 [128, 1024], P(None, 'ch'), may hold values from -0.5 to 0.5
Outputs:
- grad_input: bfloat16 [262144, 1024], P('seq', 'ch')
- grad_gate: bfloat16 [262144, 1024], P('seq', 'ch')
- grad_filter_out: float32 [128, 1024], P(None, 'ch')
- grad_filter_in: float32 [32, 128], replicated
- grad_filter_bias: float32 [128], replicated
The draws below stay inside these ranges and needn't reach their ends.
All inputs are finite; a program needn't handle non-finite values.
Results may differ from the reference program's by a relative error of at most 0.009.
Values may be sent and summed in bfloat16 or wider, within the bound.
No kernel may reach another device: no remote copies, remote signals or barrier semaphores. Data moves between devices by JAX's collectives and lax.ppermute only.
A program may use at most 128 MiB of HBM per device.

```python
import math
import jax
import jax.numpy as jnp
from jax import lax

A = 512
B = 512
D = 1024
H = 128
E = 32
L = 262144


def level_of(rng, shape, cuts, low, top_value):
    loudness, own = 1.0, jax.random.fold_in(rng, 6)
    for position, shards_of in cuts:
        heights = jnp.exp(jax.random.uniform(jax.random.fold_in(own, position), (shards_of,), jnp.float32, low / len(cuts), top_value / len(cuts)))
        loudness = loudness * jnp.repeat(heights, shape[position] // shards_of).reshape([-1 if axis == position else 1 for axis in range(len(shape))])
    return loudness


def bell_draw(own_key, dims, width, most, cuts=(), kind=jnp.bfloat16):
    result = width * jax.random.normal(own_key, dims, jnp.float32)
    if cuts:
        result = result * level_of(own_key, dims, cuts, -0.22, 0.18)
    return jnp.clip(result, -most, most).astype(kind)


def setup_inputs(seed: int = 0) -> dict:
    streams_of = jax.random.split(jax.random.key(seed), 13)
    gated_input = bell_draw(streams_of[0], (L, D), 1.0, 6.0, ((0, 64), (1, 4)))
    out_gate = bell_draw(streams_of[1], (L, D), 1.0, 6.0, ((0, 64), (1, 4)))
    grad_out = bell_draw(streams_of[2], (L, D), 1.0, 6.0, ((0, 64), (1, 4)))
    forward_inner = bell_draw(streams_of[3], (B, B), B ** -0.5, 0.25)
    forward_outer = bell_draw(streams_of[4], (A, A), A ** -0.5, 0.25)
    inverse_outer = bell_draw(streams_of[5], (A, A), A ** -0.5, 0.25)
    inverse_inner = bell_draw(streams_of[6], (B, B), B ** -0.5, 0.25)
    twiddle_forward = jnp.clip(0.5 + 1.0 * jax.random.uniform(streams_of[7], (A, B), jnp.float32) ** level_of(streams_of[7], (A, B), ((1, 64),), -0.2, 0.2), 0.5, 1.5)
    twiddle_inverse = jnp.clip(0.5 + 1.0 * jax.random.uniform(streams_of[8], (A, B), jnp.float32) ** level_of(streams_of[8], (A, B), ((1, 64),), -0.2, 0.2), 0.5, 1.5)
    filter_in = bell_draw(streams_of[9], (E, H), E ** -0.5, 1.0, (), jnp.float32)
    filter_bias = jnp.clip(jax.random.uniform(streams_of[10], (H,), jnp.float32, -3.140625, 3.140625), -3.140625, 3.140625)
    filter_out = bell_draw(streams_of[11], (H, D), H ** -0.5, 0.5, ((1, 4),))
    return {"gated_input": gated_input, "out_gate": out_gate, "grad_out": grad_out, "forward_inner": forward_inner, "forward_outer": forward_outer, "inverse_outer": inverse_outer, "inverse_inner": inverse_inner, "twiddle_forward": twiddle_forward, "twiddle_inverse": twiddle_inverse, "filter_in": filter_in, "filter_bias": filter_bias, "filter_out": filter_out}


def features(rows_index, cols_index, feature_count, size_a, size_b):
    halves = feature_count // 2
    series = jnp.arange(halves, dtype=jnp.int32)
    row_freq = (7 * series + 1) % size_a
    col_freq = (13 * series + 3) % size_b
    row_phase = ((rows_index[:, None, None] * row_freq[None, None, :]) % size_a).astype(jnp.float32) / size_a
    col_phase = ((cols_index[None, :, None] * col_freq[None, None, :]) % size_b).astype(jnp.float32) / size_b
    angles = 2.0 * math.pi * (row_phase + col_phase)
    return jnp.concatenate([jnp.sin(angles), jnp.cos(angles)], axis=-1)


def rounded(value):
    return lax.optimization_barrier(value.astype(jnp.bfloat16)).astype(jnp.float32)


def reference(gated_input, out_gate, grad_out, forward_inner, forward_outer, inverse_outer, inverse_inner, twiddle_forward, twiddle_inverse, filter_in, filter_bias, filter_out):
    highest = lax.Precision.HIGHEST
    inputs = gated_input.reshape(A, B, D)
    gates = out_gate.reshape(A, B, D)
    upstream = grad_out.reshape(A, B, D)
    inner_one = forward_inner.astype(jnp.float32)
    outer_one = forward_outer.astype(jnp.float32)
    outer_two = inverse_outer.astype(jnp.float32)
    inner_two = inverse_inner.astype(jnp.float32)
    feature_map = features(jnp.arange(A, dtype=jnp.int32), jnp.arange(B, dtype=jnp.int32), E, A, B)
    preact = jnp.einsum('jke,eh->jkh', feature_map, filter_in.astype(jnp.float32), precision=highest) + filter_bias.astype(jnp.float32)
    hidden = rounded(jnp.sin(preact))
    block_width = math.gcd(D, 64)
    block_count = D // block_width

    def step(carry, block_index):
        start = block_index * block_width

        def take(array):
            return lax.dynamic_slice_in_dim(array, start, block_width, 2).astype(jnp.float32)

        inputs_part = take(inputs)
        gates_part = take(gates)
        upstream_part = take(upstream)
        weight_part = lax.dynamic_slice_in_dim(filter_out, start, block_width, 1).astype(jnp.float32)
        kernel = jnp.einsum('jkh,hc->jkc', hidden, weight_part, precision=highest)
        first = rounded(jnp.einsum('kb,abc->akc', inner_one, inputs_part, precision=highest))
        turned = rounded(twiddle_forward[:, :, None] * first)
        spectrum = rounded(jnp.einsum('ja,akc->jkc', outer_one, turned, precision=highest))
        filtered = rounded(kernel * spectrum)
        back = rounded(twiddle_inverse[:, :, None] * jnp.einsum('aj,jkc->akc', outer_two, filtered, precision=highest))
        mixed = jnp.einsum('bk,akc->abc', inner_two, back, precision=highest)
        grad_gate = (upstream_part * mixed).astype(jnp.bfloat16)
        grad_mixed = rounded(gates_part * upstream_part)
        grad_back = rounded(jnp.einsum('bk,abc->akc', inner_two, grad_mixed, precision=highest))
        grad_turned_back = rounded(twiddle_inverse[:, :, None] * grad_back)
        grad_filtered = jnp.einsum('aj,akc->jkc', outer_two, grad_turned_back, precision=highest)
        grad_kernel = rounded(grad_filtered * spectrum)
        grad_spectrum = rounded(grad_filtered * kernel)
        grad_first = rounded(twiddle_forward[:, :, None] * jnp.einsum('ja,jkc->akc', outer_one, grad_spectrum, precision=highest))
        grad_input = jnp.einsum('kb,akc->abc', inner_one, grad_first, precision=highest).astype(jnp.bfloat16)
        weight_grad = jnp.einsum('jkh,jkc->hc', hidden, grad_kernel, precision=highest) / A
        hidden_part = jnp.einsum('jkc,hc->jkh', grad_kernel, weight_part, precision=highest)
        return carry + hidden_part, (grad_input, grad_gate, weight_grad)

    start_carry = jnp.zeros((A, B, H), jnp.float32)
    hidden_total, stacked = lax.scan(step, start_carry, jnp.arange(block_count, dtype=jnp.int32))
    input_blocks, gate_blocks, weight_blocks = stacked
    grad_preact = hidden_total * jnp.cos(preact)
    grad_filter_in = jnp.einsum('jke,jkh->eh', feature_map, grad_preact, precision=highest) / A
    grad_filter_bias = jnp.sum(grad_preact, axis=(0, 1)) / A
    grad_input = jnp.moveaxis(input_blocks, 0, 2).reshape(A * B, D)
    grad_gate = jnp.moveaxis(gate_blocks, 0, 2).reshape(A * B, D)
    grad_filter_out = jnp.moveaxis(weight_blocks, 0, 1).reshape(H, D)
    return grad_input, grad_gate, grad_filter_out, grad_filter_in, grad_filter_bias
```

```python
import functools
import math

import jax
import jax.numpy as jnp
import numpy as np
from jax import lax
from jax.experimental import pallas as pl
from jax.experimental.pallas import tpu as pltpu
from jax.sharding import PartitionSpec as P

F32 = jnp.float32
BF16 = jnp.bfloat16
MIB = 1 << 20
PARTS = 64
ROWS = 8
OUTER_LIMIT = 40
CHUNKS = 4
TABLE = 40


def dot(x, y, precision=None):
    return lax.dot_general(
        x, y, (((1,), (0,)), ((), ())), precision=precision, preferred_element_type=F32
    )


def full(shape, buffers=1):
    return pl.BlockSpec(
        shape, lambda *_: (0,) * len(shape), pipeline_mode=pl.Buffered(buffers)
    )


def outer_table(size, halves):
    series = np.arange(halves)
    phase = (np.arange(size)[:, None] * ((7 * series + 1) % size)[None, :]) % size
    angles = 2.0 * np.pi * phase / size
    table = np.zeros((size, TABLE), np.float32)
    table[:, :halves] = np.sin(angles)
    table[:, halves : 2 * halves] = np.cos(angles)
    table[:, 2 * halves] = 1.0
    return table


def inner_kernel(u_hbm, g_hbm, dy_hbm, fi_hbm, ii_hbm, o_hbm, u_ref, g_ref, dy_ref, fi_ref, ii_ref, o_ref, in_sem, out_sem):
    size, channels = u_ref.shape[1:]
    pairs = ROWS // 2
    copies = {}

    def fetch(key, source, target):
        copies[key] = pltpu.make_async_copy(source, target, in_sem.at[len(copies)])
        copies[key].start()

    fetch("fi", fi_hbm, fi_ref)
    for p in range(pairs):
        at = pl.ds(2 * p, 2)
        fetch(("u", p), u_hbm.at[at], u_ref.at[at])
    fetch("ii", ii_hbm, ii_ref)
    for p in range(pairs):
        at = pl.ds(2 * p, 2)
        fetch(("g", p), g_hbm.at[at], g_ref.at[at])
        fetch(("dy", p), dy_hbm.at[at], dy_ref.at[at])

    sends = []

    def emit(which, p, matrix, blocks):
        at = pl.ds(2 * ROWS * p, 2 * ROWS)
        parts = [dot(matrix, block).reshape(PARTS, 1, ROWS, channels) for block in blocks]
        value = jnp.concatenate(parts, 1).reshape(PARTS, 2 * ROWS, channels).astype(BF16)
        o_ref[:, which, 2 * ROWS * p : 2 * ROWS * (p + 1), :] = value
        sends.append(pltpu.make_async_copy(o_ref.at[:, which, at, :], o_hbm.at[:, which, at, :], out_sem.at[len(sends)]))
        sends[-1].start()

    copies["fi"].wait()
    for p in range(pairs):
        copies["u", p].wait()
        emit(0, p, fi_ref[...], [u_ref[2 * p], u_ref[2 * p + 1]])
    copies["ii"].wait()
    turned = ii_ref[...].astype(F32).T.astype(BF16)
    for p in range(pairs):
        copies["g", p].wait()
        copies["dy", p].wait()
        mixed = [
            (g_ref[i].astype(F32) * dy_ref[i].astype(F32)).astype(BF16)
            for i in (2 * p, 2 * p + 1)
        ]
        emit(1, p, turned, mixed)
    for send in sends:
        send.wait()


def filter_kernel(col_ref, tab_ref, fin_ref, bias_ref, hid_ref, hidt_ref, cos_ref, q_ref):
    step = pl.program_id(0)
    size = tab_ref.shape[0]
    hidden = bias_ref.shape[1]
    halves = fin_ref.shape[0] // 2
    col = col_ref[0] + step
    series = lax.broadcasted_iota(jnp.int32, (halves, hidden), 0)
    phase = (((13 * series + 3) % size) * col) % size
    angle = phase.astype(F32) * (2.0 * math.pi / size)
    sq, cq = jnp.sin(angle), jnp.cos(angle)
    q_ref[0, :halves] = cq
    q_ref[0, halves:] = sq
    ws, wc = fin_ref[:halves], fin_ref[halves:]
    weights = jnp.concatenate(
        [
            cq * ws - sq * wc,
            sq * ws + cq * wc,
            bias_ref[...],
            jnp.zeros((TABLE - 2 * halves - 1, hidden), F32),
        ],
        0,
    )
    preact = dot(tab_ref[...], weights, lax.Precision.HIGHEST)
    value = jnp.sin(preact)
    hid_ref[0] = value.astype(BF16)
    hidt_ref[0] = value.T.astype(BF16)
    cos_ref[0] = jnp.cos(preact)


def outer_kernel(
    r_hbm, fo_ref, fot_ref, io_ref, iot_ref, w_ref, wt_ref, tabt_ref, tf_ref, ti_ref,
    hid_hbm, hidt_hbm, cos_hbm, q_ref,
    o_hbm, s_ref, x_ref, y_ref, wire_ref, hid_ref, hidt_ref, cos_ref, in_sem, gen_sem, out_sem,
):
    size = fo_ref.shape[0]
    hidden, channels = w_ref.shape
    lanes = x_ref.shape[2]
    halves = q_ref.shape[1] // 2
    rows = wire_ref.shape[2]
    split = channels // lanes
    chunk = PARTS // CHUNKS

    def moved(source, target, sem):
        copies = []
        for which in (0, 1):
            for c in range(CHUNKS):
                at = pl.ds(c * chunk, chunk)
                copies.append(pltpu.make_async_copy(source.at[at, which], target.at[at, which], sem.at[len(copies)]))
        return copies

    loads = moved(r_hbm, wire_ref, in_sem)
    for load in loads:
        load.start()
    generated = [
        pltpu.make_async_copy(source, target, gen_sem.at[i])
        for i, (source, target) in enumerate(((hid_hbm, hid_ref), (hidt_hbm, hidt_ref), (cos_hbm, cos_ref)))
    ]
    for copy in generated:
        copy.start()

    for which, ref in ((0, x_ref), (1, y_ref)):
        for c in range(CHUNKS):
            loads[which * CHUNKS + c].wait()
            for part in range(c * chunk, (c + 1) * chunk):
                for i in range(split):
                    ref[i, part * rows : (part + 1) * rows] = wire_ref[part, which, :, i * lanes : (i + 1) * lanes].astype(F32)
    for copy in generated:
        copy.wait()

    weight = jnp.zeros((hidden, channels), F32)
    layer = [jnp.zeros((halves, hidden), F32)] * 2
    bias = jnp.zeros((TABLE - 2 * halves, hidden), F32)
    pending = []
    for k in range(ROWS):
        mine = pl.ds(k, size, stride=ROWS)
        tf = jnp.broadcast_to(tf_ref[:, k : k + 1], (size, lanes))
        ti = jnp.broadcast_to(ti_ref[:, k : k + 1], (size, lanes))

        def load(ref, scale):
            return jnp.concatenate([(scale * ref[i, mine, :]).astype(BF16) for i in range(split)], 1)

        def store(ref, scale, value):
            for i in range(split):
                ref[i, mine, :] = scale * value[:, i * lanes : (i + 1) * lanes]

        spectrum = dot(fo_ref[...], load(x_ref, tf)).astype(BF16).astype(F32)
        grad_filtered = dot(iot_ref[...], load(y_ref, ti))
        kernel = dot(hid_ref[k], w_ref[...])
        store(x_ref, ti, dot(io_ref[...], (kernel * spectrum).astype(BF16)))
        store(y_ref, tf, dot(fot_ref[...], (grad_filtered * kernel).astype(BF16)))
        grad_kernel = (grad_filtered * spectrum).astype(BF16)
        weight = weight + dot(hidt_ref[k], grad_kernel)
        pending.append(dot(grad_kernel, wt_ref[...]) * cos_ref[k])
        if len(pending) == 2:
            grad_preact = jnp.concatenate(pending, 1)
            pending = []
            high = grad_preact.astype(BF16)
            low = (grad_preact - high.astype(F32)).astype(BF16)
            upper = dot(tabt_ref[...], high)
            moments = upper[:TABLE] + upper[TABLE:] + dot(tabt_ref[...], low)[:TABLE]
            for i in range(2):
                part = moments[:, i * hidden : (i + 1) * hidden]
                cq, sq = q_ref[k - 1 + i, :halves], q_ref[k - 1 + i, halves:]
                ms, mc = part[:halves], part[halves : 2 * halves]
                layer = [layer[0] + cq * ms + sq * mc, layer[1] + cq * mc - sq * ms]
                bias = bias + part[2 * halves :]

    sends = moved(wire_ref, o_hbm, out_sem)
    for which, ref in ((0, x_ref), (1, y_ref)):
        for c in range(CHUNKS):
            for part in range(c * chunk, (c + 1) * chunk):
                for i in range(split):
                    wire_ref[part, which, :, i * lanes : (i + 1) * lanes] = ref[i, part * rows : (part + 1) * rows].astype(BF16)
            sends[which * CHUNKS + c].start()

    scale = 1.0 / size
    for i in range(split):
        s_ref[i * hidden : (i + 1) * hidden] = weight[:, i * lanes : (i + 1) * lanes] * scale
    s_ref[split * hidden :] = jnp.concatenate(layer + [bias], 0) * scale
    for send in sends:
        send.wait()


def tokens_kernel(x_hbm, dy_ref, ii_ref, fi_ref, gi_hbm, gg_hbm, x_ref, gi_ref, gg_ref, in_sem, out_sem):
    size, channels = dy_ref.shape[1:]
    pairs = ROWS // 2
    loads, sends = {}, []
    for which in (0, 1):
        for p in range(pairs):
            at = pl.ds(2 * ROWS * p, 2 * ROWS)
            loads[which, p] = pltpu.make_async_copy(x_hbm.at[:, which, at, :], x_ref.at[:, which, at, :], in_sem.at[len(loads)])
            loads[which, p].start()

    def operands(which, p):
        loads[which, p].wait()
        value = x_ref[:, which, 2 * ROWS * p : 2 * ROWS * (p + 1), :].astype(F32)
        return [value[:, i * ROWS : (i + 1) * ROWS].reshape(size, channels).astype(BF16) for i in range(2)]

    def emit(source, target, p):
        at = pl.ds(2 * p, 2)
        sends.append(pltpu.make_async_copy(source.at[at], target.at[at], out_sem.at[len(sends)]))
        sends[-1].start()

    for p in range(pairs):
        for i, back in enumerate(operands(0, p)):
            mixed = dot(ii_ref[...], back)
            gg_ref[2 * p + i] = (dy_ref[2 * p + i].astype(F32) * mixed).astype(BF16)
        emit(gg_ref, gg_hbm, p)
    turned = fi_ref[...].astype(F32).T.astype(BF16)
    for p in range(pairs):
        for i, first in enumerate(operands(1, p)):
            gi_ref[2 * p + i] = dot(turned, first).astype(BF16)
        emit(gi_ref, gi_hbm, p)
    for send in sends:
        send.wait()


def pair_kernel(one_ref, other_ref, after_ref, o_ref):
    o_ref[...] = one_ref[...] + other_ref[...]


def finish_kernel(v_ref, a_ref, b_ref, c_ref, after_ref, w_ref, l_ref, b_out_ref):
    hidden, channels = w_ref.shape
    features = l_ref.shape[0]
    lanes = v_ref.shape[1]
    total = (v_ref[...] + a_ref[...]) + (b_ref[...] + c_ref[...])
    split = channels // lanes
    for i in range(split):
        w_ref[:, i * lanes : (i + 1) * lanes] = total[i * hidden : (i + 1) * hidden]
    l_ref[...] = total[split * hidden : split * hidden + features]
    b_out_ref[...] = total[split * hidden + features : split * hidden + features + 1]


def params(limit, axes=1):
    return pltpu.CompilerParams(
        vmem_limit_bytes=limit * MIB, dimension_semantics=("arbitrary",) * axes
    )


def exchanged(value, axis, count, step):
    return lax.ppermute(value, axis, [(i, i ^ step) for i in range(count)])


def doubled(value, axis, count, steps):
    for step in steps:
        value = value + exchanged(value, axis, count, step)
    return value


def shards(
    gated_input,
    out_gate,
    grad_out,
    forward_inner,
    forward_outer,
    inverse_outer,
    inverse_inner,
    twiddle_forward,
    twiddle_inverse,
    filter_in,
    filter_bias,
    filter_out,
):
    size = forward_outer.shape[0]
    channels = gated_input.shape[1]
    hidden = filter_in.shape[1]
    features = filter_in.shape[0]
    lanes = 128
    tokens = (ROWS, size, channels)
    inputs, gates, upstream = (x.reshape(tokens) for x in (gated_input, out_gate, grad_out))
    square = (size, size)
    pair = pl.BlockSpec((2, size, channels), lambda p: (p, 0, 0))
    wire = (PARTS, 2, ROWS * ROWS, channels)
    wire_pair = pl.BlockSpec((PARTS, 2, 2 * ROWS, channels), lambda p: (0, 0, p, 0))

    anywhere = pl.BlockSpec(memory_space=pltpu.HBM)
    inside = pl.BlockSpec(memory_space=pltpu.VMEM)
    sent = pl.pallas_call(
        inner_kernel,
        out_shape=jax.ShapeDtypeStruct(wire, BF16),
        in_specs=[anywhere] * 5,
        out_specs=anywhere,
        scratch_shapes=[pltpu.VMEM(tokens, BF16)] * 3
        + [pltpu.VMEM(square, BF16)] * 2
        + [pltpu.VMEM(wire, BF16), pltpu.SemaphoreType.DMA((2 + 3 * ROWS // 2,)), pltpu.SemaphoreType.DMA((ROWS,))],
        compiler_params=pltpu.CompilerParams(vmem_limit_bytes=62 * MIB),
        cost_estimate=pl.CostEstimate(flops=4 * ROWS * size * size * channels, bytes_accessed=10 * MIB, transcendentals=0),
        name="inner_transforms",
    )(inputs, gates, upstream, forward_inner, inverse_inner)

    column = lax.axis_index("seq").astype(jnp.int32).reshape(1) * ROWS
    sent, column = lax.optimization_barrier((sent, column))
    received = lax.all_to_all(sent, "seq", split_axis=0, concat_axis=0, tiled=True)

    table = outer_table(size, features // 2)
    each = lambda *shape: pl.BlockSpec((1,) + shape, lambda k, *_: (k,) + (0,) * len(shape))
    made = [
        ((size, hidden), BF16),
        ((hidden, size), BF16),
        ((size, hidden), F32),
        ((features, hidden), F32),
    ]
    generated = pl.pallas_call(
        filter_kernel,
        grid_spec=pltpu.PrefetchScalarGridSpec(
            num_scalar_prefetch=1,
            grid=(ROWS,),
            in_specs=[full((size, TABLE)), full((features, hidden)), full((1, hidden))],
            out_specs=[each(*shape) for shape, _ in made],
        ),
        out_shape=[jax.ShapeDtypeStruct((ROWS,) + shape, kind) for shape, kind in made],
        compiler_params=params(32),
        cost_estimate=pl.CostEstimate(flops=40 * MIB, bytes_accessed=9 * MIB, transcendentals=2 * MIB),
        name="filter_generator",
    )(column, table, filter_in, filter_bias.reshape(1, hidden))

    small = (2 * hidden + TABLE, lanes)
    high = table.T.astype(BF16)
    low = (table.T - high.astype(np.float32)).astype(BF16)
    returned, partial = pl.pallas_call(
        outer_kernel,
        out_shape=[jax.ShapeDtypeStruct(wire, BF16), jax.ShapeDtypeStruct(small, F32)],
        in_specs=[anywhere] + [inside] * 9 + [anywhere] * 3 + [inside],
        out_specs=[anywhere, inside],
        scratch_shapes=[pltpu.VMEM((channels // lanes, ROWS * size, lanes), F32)] * 2
        + [pltpu.VMEM(wire, BF16)]
        + [pltpu.VMEM((ROWS,) + shape, kind) for shape, kind in made[:3]]
        + [pltpu.SemaphoreType.DMA((count,)) for count in (2 * CHUNKS, 3, 2 * CHUNKS)],
        compiler_params=pltpu.CompilerParams(vmem_limit_bytes=OUTER_LIMIT * MIB),
        cost_estimate=pl.CostEstimate(flops=10 * ROWS * size * size * channels, bytes_accessed=18 * MIB, transcendentals=0),
        name="outer_transforms",
    )(received, forward_outer, forward_outer.T, inverse_outer, inverse_outer.T, filter_out, filter_out.T, np.concatenate([high, low], 0), twiddle_forward, twiddle_inverse, *generated)

    arrived = lax.all_to_all(returned, "seq", split_axis=0, concat_axis=0, tiled=True)

    layer = doubled(partial[2 * hidden :], "ch", 4, (1, 2))
    total = jnp.concatenate([partial[: 2 * hidden], layer], 0)
    total = doubled(total, "seq", PARTS, (1, 16, 32))
    total = pl.pallas_call(
        pair_kernel,
        out_shape=jax.ShapeDtypeStruct(small, F32),
        in_specs=[inside, inside, anywhere],
        out_specs=inside,
        name="pair_sum",
    )(total, exchanged(total, "seq", PARTS, 2), arrived)
    others = [exchanged(total, "seq", PARTS, step) for step in (4, 8, 12)]

    grad_input, grad_gate = pl.pallas_call(
        tokens_kernel,
        out_shape=[jax.ShapeDtypeStruct(tokens, BF16)] * 2,
        in_specs=[anywhere, inside, inside, inside],
        out_specs=[anywhere] * 2,
        scratch_shapes=[pltpu.VMEM(wire, BF16), pltpu.VMEM(tokens, BF16), pltpu.VMEM(tokens, BF16), pltpu.SemaphoreType.DMA((ROWS,)), pltpu.SemaphoreType.DMA((ROWS,))],
        compiler_params=pltpu.CompilerParams(vmem_limit_bytes=32 * MIB),
        cost_estimate=pl.CostEstimate(flops=4 * ROWS * size * size * channels, bytes_accessed=10 * MIB, transcendentals=0),
        name="token_gradients",
    )(arrived, upstream, inverse_inner, forward_inner)
    weight_grad, layer_grad, bias_grad = pl.pallas_call(
        finish_kernel,
        out_shape=[
            jax.ShapeDtypeStruct((hidden, channels), F32),
            jax.ShapeDtypeStruct((features, hidden), F32),
            jax.ShapeDtypeStruct((1, hidden), F32),
        ],
        in_specs=[inside] * 4 + [anywhere],
        name="weight_gradients",
    )(total, *others, grad_gate)
    flat = (ROWS * size, channels)
    return grad_input.reshape(flat), grad_gate.reshape(flat), weight_grad, layer_grad, bias_grad.reshape(hidden)


def solution(mesh):
    return jax.shard_map(
        shards,
        mesh=mesh,
        in_specs=(
            P("seq", "ch"),
            P("seq", "ch"),
            P("seq", "ch"),
            P(),
            P(),
            P(),
            P(),
            P(None, "seq"),
            P(None, "seq"),
            P(),
            P(),
            P(None, "ch"),
        ),
        out_specs=(P("seq", "ch"), P("seq", "ch"), P(None, "ch"), P(), P()),
        check_vma=False,
    )
```

```python
import functools
import math

import jax
import jax.numpy as jnp
import numpy as np
from jax import lax
from jax.experimental import pallas as pl
from jax.experimental.pallas import tpu as pltpu
from jax.sharding import PartitionSpec as P

F32 = jnp.float32
BF16 = jnp.bfloat16
MIB = 1 << 20
PARTS = 64
ROWS = 8
OUTER_LIMIT = 62
CHUNKS = 4
PITCH = 520
TABLE = 48


def dot(x, y, precision=None):
    return lax.dot_general(
        x, y, (((1,), (0,)), ((), ())), precision=precision, preferred_element_type=F32
    )


def full(shape, buffers=1):
    return pl.BlockSpec(
        shape, lambda *_: (0,) * len(shape), pipeline_mode=pl.Buffered(buffers)
    )


def outer_table(size, halves):
    series = np.arange(halves)
    phase = (np.arange(size)[:, None] * ((7 * series + 1) % size)[None, :]) % size
    angles = 2.0 * np.pi * phase / size
    table = np.zeros((size, TABLE), np.float32)
    table[:, :halves] = np.sin(angles)
    table[:, halves : 2 * halves] = np.cos(angles)
    table[:, 2 * halves] = 1.0
    return table


def inner_kernel(u_hbm, g_hbm, dy_hbm, fi_hbm, ii_hbm, o_hbm, u_ref, g_ref, dy_ref, fi_ref, ii_ref, o_ref, in_sem, out_sem):
    size, channels = u_ref.shape[1:]
    pairs = ROWS // 2
    copies = {}

    def fetch(key, source, target):
        copies[key] = pltpu.make_async_copy(source, target, in_sem.at[len(copies)])
        copies[key].start()

    fetch("fi", fi_hbm, fi_ref)
    for p in range(pairs):
        at = pl.ds(2 * p, 2)
        fetch(("u", p), u_hbm.at[at], u_ref.at[at])
    fetch("ii", ii_hbm, ii_ref)
    for p in range(pairs):
        at = pl.ds(2 * p, 2)
        fetch(("g", p), g_hbm.at[at], g_ref.at[at])
        fetch(("dy", p), dy_hbm.at[at], dy_ref.at[at])

    sends = []

    def emit(which, p, matrix, blocks):
        at = pl.ds(2 * ROWS * p, 2 * ROWS)
        parts = [dot(matrix, block).reshape(PARTS, 1, ROWS, channels) for block in blocks]
        value = jnp.concatenate(parts, 1).reshape(PARTS, 2 * ROWS, channels).astype(BF16)
        o_ref[:, which, 2 * ROWS * p : 2 * ROWS * (p + 1), :] = value
        sends.append(pltpu.make_async_copy(o_ref.at[:, which, at, :], o_hbm.at[:, which, at, :], out_sem.at[len(sends)]))
        sends[-1].start()

    copies["fi"].wait()
    for p in range(pairs):
        copies["u", p].wait()
        emit(0, p, fi_ref[...], [u_ref[2 * p], u_ref[2 * p + 1]])
    copies["ii"].wait()
    turned = ii_ref[...].astype(F32).T.astype(BF16)
    for p in range(pairs):
        copies["g", p].wait()
        copies["dy", p].wait()
        mixed = [
            (g_ref[i].astype(F32) * dy_ref[i].astype(F32)).astype(BF16)
            for i in (2 * p, 2 * p + 1)
        ]
        emit(1, p, turned, mixed)
    for send in sends:
        send.wait()


def filter_kernel(col_ref, tab_ref, fin_ref, bias_ref, hid_ref, hidt_ref, cos_ref, q_ref):
    step = pl.program_id(0)
    size = tab_ref.shape[0]
    hidden = bias_ref.shape[1]
    halves = fin_ref.shape[0] // 2
    col = col_ref[0] + step
    series = lax.broadcasted_iota(jnp.int32, (halves, hidden), 0)
    phase = (((13 * series + 3) % size) * col) % size
    angle = phase.astype(F32) * (2.0 * math.pi / size)
    sq, cq = jnp.sin(angle), jnp.cos(angle)
    q_ref[0, :halves] = cq
    q_ref[0, halves:] = sq
    ws, wc = fin_ref[:halves], fin_ref[halves:]
    weights = jnp.concatenate(
        [
            cq * ws - sq * wc,
            sq * ws + cq * wc,
            bias_ref[...],
            jnp.zeros((TABLE - 2 * halves - 1, hidden), F32),
        ],
        0,
    )
    preact = dot(tab_ref[...], weights, lax.Precision.HIGHEST)
    value = jnp.sin(preact)
    hid_ref[0] = value.astype(BF16)
    hidt_ref[0] = value.T.astype(BF16)
    cos_ref[0] = jnp.cos(preact)


def outer_kernel(r_hbm, *refs):
    sources, (o_hbm, s_ref, x_ref, y_ref, out_ref, wire_ref, spec_ref), refs = refs[:13], refs[13:20], refs[20:]
    targets, (in_sem, side_sem, out_sem) = refs[:13], refs[13:]
    (fo_ref, tf_ref, w_ref, hid_ref, io_ref, ti_ref, iot_ref, fot_ref, hidt_ref, wt_ref, cos_ref, tabt_ref, q_ref) = targets
    size = fo_ref.shape[0]
    hidden, channels = w_ref.shape
    lanes = x_ref.shape[2]
    halves = q_ref.shape[1] // 2
    rows = wire_ref.shape[2]
    split = channels // lanes
    chunk = PARTS // CHUNKS

    def moved(source, target, sem):
        copies = []
        for which in (0, 1):
            for c in range(CHUNKS):
                at = pl.ds(c * chunk, chunk)
                copies.append(pltpu.make_async_copy(source.at[at, which], target.at[at, which], sem.at[len(copies)]))
        return copies

    loads = moved(r_hbm, wire_ref, in_sem)
    aside = [pltpu.make_async_copy(source, target, side_sem.at[i]) for i, (source, target) in enumerate(zip(sources, targets))]
    for copy in aside[:2] + loads[:CHUNKS] + aside[2:6] + loads[CHUNKS:] + aside[6:]:
        copy.start()
    sends = moved(wire_ref, o_hbm, out_sem)

    def spread(which, ref):
        for c in range(CHUNKS):
            loads[which * CHUNKS + c].wait()
            for part in range(c * chunk, (c + 1) * chunk):
                for i in range(split):
                    ref[i, part * rows : (part + 1) * rows] = wire_ref[part, which, :, i * lanes : (i + 1) * lanes].astype(F32)

    def send(which):
        for c in range(CHUNKS):
            for part in range(c * chunk, (c + 1) * chunk):
                for i in range(split):
                    lane = slice(i * lanes, (i + 1) * lanes)
                    value = [out_ref[i, pl.ds(part * ROWS + a, ROWS, stride=PITCH), :] for a in range(ROWS)]
                    wire_ref[part, which, :, lane] = jnp.concatenate(value, 0).astype(BF16)
            sends[which * CHUNKS + c].start()

    def load(ref, k, scale_ref):
        scale = jnp.broadcast_to(scale_ref[:, k : k + 1], (size, lanes))
        mine = pl.ds(k, size, stride=ROWS)
        return jnp.concatenate([(scale * ref[i, mine, :]).astype(BF16) for i in range(split)], 1)

    def store(k, scale_ref, value):
        scale = jnp.broadcast_to(scale_ref[:, k : k + 1], (size, lanes))
        for i in range(split):
            out_ref[i, k * PITCH : k * PITCH + size] = scale * value[:, i * lanes : (i + 1) * lanes]

    spread(0, x_ref)
    for copy in aside[:6]:
        copy.wait()
    coming = dot(fo_ref[...], load(x_ref, 0, tf_ref)).astype(BF16)
    for k in range(ROWS):
        spectrum = coming
        spec_ref[k] = spectrum
        if k + 1 < ROWS:
            coming = dot(fo_ref[...], load(x_ref, k + 1, tf_ref)).astype(BF16)
        filtered = (dot(hid_ref[k], w_ref[...]) * spectrum.astype(F32)).astype(BF16)
        store(k, ti_ref, dot(io_ref[...], filtered))
    spread(1, y_ref)
    send(0)
    for copy in aside[6:]:
        copy.wait()

    weight = jnp.zeros((hidden, channels), F32)
    layer = [jnp.zeros((halves, hidden), F32)] * 2
    bias = jnp.zeros((TABLE - 2 * halves, hidden), F32)
    pending = []
    coming = dot(iot_ref[...], load(y_ref, 0, ti_ref))
    for k in range(ROWS):
        grad_filtered = coming
        if k + 1 < ROWS:
            coming = dot(iot_ref[...], load(y_ref, k + 1, ti_ref))
        kernel = dot(hid_ref[k], w_ref[...])
        store(k, tf_ref, dot(fot_ref[...], (grad_filtered * kernel).astype(BF16)))
        grad_kernel = (grad_filtered * spec_ref[k].astype(F32)).astype(BF16)
        weight = weight + dot(hidt_ref[k], grad_kernel)
        pending.append(dot(grad_kernel, wt_ref[...]) * cos_ref[k])
        if len(pending) == 2:
            grad_preact = jnp.concatenate(pending, 1)
            pending = []
            high = grad_preact.astype(BF16)
            low = (grad_preact - high.astype(F32)).astype(BF16)
            upper = dot(tabt_ref[...], high)
            moments = upper[:TABLE] + upper[TABLE:] + dot(tabt_ref[...], low)[:TABLE]
            for i in range(2):
                part = moments[:, i * hidden : (i + 1) * hidden]
                cq, sq = q_ref[k - 1 + i, :halves], q_ref[k - 1 + i, halves:]
                ms, mc = part[:halves], part[halves : 2 * halves]
                layer = [layer[0] + cq * ms + sq * mc, layer[1] + cq * mc - sq * ms]
                bias = bias + part[2 * halves :]
    send(1)

    scale = 1.0 / size
    for i in range(split):
        s_ref[i * hidden : (i + 1) * hidden] = weight[:, i * lanes : (i + 1) * lanes] * scale
    s_ref[split * hidden :] = jnp.concatenate(layer + [bias], 0) * scale
    for copy in sends:
        copy.wait()


def tokens_kernel(x_hbm, dy_ref, ii_ref, fi_ref, gi_hbm, gg_hbm, x_ref, gi_ref, gg_ref, in_sem, out_sem):
    size, channels = dy_ref.shape[1:]
    pairs = ROWS // 2
    loads, sends = {}, []
    for which in (0, 1):
        for p in range(pairs):
            at = pl.ds(2 * ROWS * p, 2 * ROWS)
            loads[which, p] = pltpu.make_async_copy(x_hbm.at[:, which, at, :], x_ref.at[:, which, at, :], in_sem.at[len(loads)])
            loads[which, p].start()

    def operands(which, p):
        loads[which, p].wait()
        value = x_ref[:, which, 2 * ROWS * p : 2 * ROWS * (p + 1), :].astype(F32)
        return [value[:, i * ROWS : (i + 1) * ROWS].reshape(size, channels).astype(BF16) for i in range(2)]

    def emit(source, target, p):
        at = pl.ds(2 * p, 2)
        sends.append(pltpu.make_async_copy(source.at[at], target.at[at], out_sem.at[len(sends)]))
        sends[-1].start()

    for p in range(pairs):
        for i, back in enumerate(operands(0, p)):
            mixed = dot(ii_ref[...], back)
            gg_ref[2 * p + i] = (dy_ref[2 * p + i].astype(F32) * mixed).astype(BF16)
        emit(gg_ref, gg_hbm, p)
    turned = fi_ref[...].astype(F32).T.astype(BF16)
    for p in range(pairs):
        for i, first in enumerate(operands(1, p)):
            gi_ref[2 * p + i] = dot(turned, first).astype(BF16)
        emit(gi_ref, gi_hbm, p)
    for send in sends:
        send.wait()


def finish_kernel(core_ref, mine_ref, other_ref, w_ref, l_ref, b_ref):
    hidden = w_ref.shape[0]
    features = l_ref.shape[0]
    half, lanes = mine_ref.shape
    mine, other = mine_ref[...], other_ref[...]
    lower = jnp.where(core_ref[0] == 0, mine, other)
    upper = jnp.where(core_ref[0] == 0, other, mine)
    w_ref[:, :lanes] = lower[:hidden]
    w_ref[: half - hidden, lanes:] = lower[hidden:]
    w_ref[half - hidden :, lanes:] = upper[: 2 * hidden - half]
    l_ref[...] = upper[2 * hidden - half : 2 * hidden - half + features]
    b_ref[...] = upper[2 * hidden - half + features : 2 * hidden - half + features + 1]


def after(value, *others):
    return lax.optimization_barrier((value,) + others)[0]


def params(limit, axes=1):
    return pltpu.CompilerParams(
        vmem_limit_bytes=limit * MIB, dimension_semantics=("arbitrary",) * axes
    )


def exchanged(value, axis, count, step):
    return lax.ppermute(value, axis, [(i, i ^ step) for i in range(count)])


def doubled(value, axis, count, steps):
    for step in steps:
        value = value + exchanged(value, axis, count, step)
    return value


def shards(
    gated_input,
    out_gate,
    grad_out,
    forward_inner,
    forward_outer,
    inverse_outer,
    inverse_inner,
    twiddle_forward,
    twiddle_inverse,
    filter_in,
    filter_bias,
    filter_out,
):
    size = forward_outer.shape[0]
    channels = gated_input.shape[1]
    hidden = filter_in.shape[1]
    features = filter_in.shape[0]
    lanes = 128
    tokens = (ROWS, size, channels)
    inputs, gates, upstream = (x.reshape(tokens) for x in (gated_input, out_gate, grad_out))
    square = (size, size)
    pair = pl.BlockSpec((2, size, channels), lambda p: (p, 0, 0))
    wire = (PARTS, 2, ROWS * ROWS, channels)
    wire_pair = pl.BlockSpec((PARTS, 2, 2 * ROWS, channels), lambda p: (0, 0, p, 0))

    anywhere = pl.BlockSpec(memory_space=pltpu.HBM)
    inside = pl.BlockSpec(memory_space=pltpu.VMEM)
    sent = pl.pallas_call(
        inner_kernel,
        out_shape=jax.ShapeDtypeStruct(wire, BF16),
        in_specs=[anywhere] * 5,
        out_specs=anywhere,
        scratch_shapes=[pltpu.VMEM(tokens, BF16)] * 3
        + [pltpu.VMEM(square, BF16)] * 2
        + [pltpu.VMEM(wire, BF16), pltpu.SemaphoreType.DMA((2 + 3 * ROWS // 2,)), pltpu.SemaphoreType.DMA((ROWS,))],
        compiler_params=pltpu.CompilerParams(vmem_limit_bytes=62 * MIB),
        cost_estimate=pl.CostEstimate(flops=4 * ROWS * size * size * channels, bytes_accessed=10 * MIB, transcendentals=0),
        name="inner_transforms",
    )(inputs, gates, upstream, forward_inner, inverse_inner)

    column = lax.axis_index("seq").astype(jnp.int32).reshape(1) * ROWS
    sent, column = lax.optimization_barrier((sent, column))
    received = lax.all_to_all(sent, "seq", split_axis=0, concat_axis=0, tiled=True)

    table = outer_table(size, features // 2)
    each = lambda *shape: pl.BlockSpec((1,) + shape, lambda k, *_: (k,) + (0,) * len(shape))
    made = [
        ((size, hidden), BF16),
        ((hidden, size), BF16),
        ((size, hidden), F32),
        ((features, hidden), F32),
    ]
    generated = pl.pallas_call(
        filter_kernel,
        grid_spec=pltpu.PrefetchScalarGridSpec(
            num_scalar_prefetch=1,
            grid=(ROWS,),
            in_specs=[full((size, TABLE)), full((features, hidden)), full((1, hidden))],
            out_specs=[each(*shape) for shape, _ in made],
        ),
        out_shape=[jax.ShapeDtypeStruct((ROWS,) + shape, kind) for shape, kind in made],
        compiler_params=params(32),
        cost_estimate=pl.CostEstimate(flops=40 * MIB, bytes_accessed=9 * MIB, transcendentals=2 * MIB),
        name="filter_generator",
    )(column, table, filter_in, filter_bias.reshape(1, hidden))

    small = (2 * hidden + TABLE, lanes)
    high = table.T.astype(BF16)
    low = (table.T - high.astype(np.float32)).astype(BF16)
    hid, hidt, cosine, turns = generated
    aside = [
        forward_outer, twiddle_forward, filter_out, hid, inverse_outer, twiddle_inverse,
        inverse_outer.T, forward_outer.T, hidt, filter_out.T, cosine, np.concatenate([high, low], 0), turns,
    ]
    returned, partial = pl.pallas_call(
        outer_kernel,
        out_shape=[jax.ShapeDtypeStruct(wire, BF16), jax.ShapeDtypeStruct(small, F32)],
        in_specs=[anywhere] * 14,
        out_specs=[anywhere, inside],
        scratch_shapes=[pltpu.VMEM((channels // lanes, ROWS * size, lanes), F32)] * 2
        + [pltpu.VMEM((channels // lanes, ROWS * PITCH, lanes), F32)]
        + [pltpu.VMEM(wire, BF16), pltpu.VMEM(tokens, BF16)]
        + [pltpu.VMEM(array.shape, array.dtype) for array in aside]
        + [pltpu.SemaphoreType.DMA((count,)) for count in (2 * CHUNKS, len(aside), 2 * CHUNKS)],
        compiler_params=pltpu.CompilerParams(vmem_limit_bytes=OUTER_LIMIT * MIB),
        cost_estimate=pl.CostEstimate(flops=10 * ROWS * size * size * channels, bytes_accessed=18 * MIB, transcendentals=0),
        name="outer_transforms",
    )(received, *aside)

    arrived = lax.all_to_all(returned, "seq", split_axis=0, concat_axis=0, tiled=True)

    layer = doubled(partial[2 * hidden :], "ch", 4, (1, 2))
    total = jnp.concatenate([partial[: 2 * hidden], layer], 0)
    half = small[0] // 2
    lower, upper = total[:half], total[half:]
    core = lax.axis_index("seq") % 2
    mine = jnp.where(core == 0, lower, upper)
    mine = mine + exchanged(jnp.where(core == 0, upper, lower), "seq", PARTS, 1)
    mine = doubled(mine, "seq", PARTS, (16, 32, 8))
    other = exchanged(mine, "seq", PARTS, 4)

    grad_input, grad_gate = pl.pallas_call(
        tokens_kernel,
        out_shape=[jax.ShapeDtypeStruct(tokens, BF16)] * 2,
        in_specs=[anywhere, inside, inside, inside],
        out_specs=[anywhere] * 2,
        scratch_shapes=[pltpu.VMEM(wire, BF16), pltpu.VMEM(tokens, BF16), pltpu.VMEM(tokens, BF16), pltpu.SemaphoreType.DMA((ROWS,)), pltpu.SemaphoreType.DMA((ROWS,))],
        compiler_params=pltpu.CompilerParams(vmem_limit_bytes=32 * MIB),
        cost_estimate=pl.CostEstimate(flops=4 * ROWS * size * size * channels, bytes_accessed=10 * MIB, transcendentals=0),
        name="token_gradients",
    )(arrived, upstream, inverse_inner, forward_inner)
    mine = doubled(mine + after(other, grad_gate), "seq", PARTS, (2,))
    weight_grad, layer_grad, bias_grad = pl.pallas_call(
        finish_kernel,
        out_shape=[
            jax.ShapeDtypeStruct((hidden, channels), F32),
            jax.ShapeDtypeStruct((features, hidden), F32),
            jax.ShapeDtypeStruct((1, hidden), F32),
        ],
        in_specs=[pl.BlockSpec(memory_space=pltpu.SMEM), inside, inside],
        name="weight_gradients",
    )(core.astype(jnp.int32).reshape(1), mine, exchanged(mine, "seq", PARTS, 1))
    flat = (ROWS * size, channels)
    return grad_input.reshape(flat), grad_gate.reshape(flat), weight_grad, layer_grad, bias_grad.reshape(hidden)


def solution(mesh):
    return jax.shard_map(
        shards,
        mesh=mesh,
        in_specs=(
            P("seq", "ch"),
            P("seq", "ch"),
            P("seq", "ch"),
            P(),
            P(),
            P(),
            P(),
            P(None, "seq"),
            P(None, "seq"),
            P(),
            P(),
            P(None, "ch"),
        ),
        out_specs=(P("seq", "ch"), P("seq", "ch"), P(None, "ch"), P(), P()),
        check_vma=False,
    )
```

```python
import functools
import math

import jax
import jax.numpy as jnp
import numpy as np
from jax import lax
from jax.experimental import pallas as pl
from jax.experimental.pallas import tpu as pltpu
from jax.sharding import PartitionSpec as P

F32 = jnp.float32
BF16 = jnp.bfloat16
MIB = 1 << 20
PARTS = 64
ROWS = 8
OUTER_LIMIT = 62
CHUNKS = 8
PITCH = 521
TABLE = 48


def dot(x, y, precision=None):
    return lax.dot_general(
        x, y, (((1,), (0,)), ((), ())), precision=precision, preferred_element_type=F32
    )


def full(shape, buffers=1):
    return pl.BlockSpec(
        shape, lambda *_: (0,) * len(shape), pipeline_mode=pl.Buffered(buffers)
    )


def outer_table(size, halves):
    series = np.arange(halves)
    phase = (np.arange(size)[:, None] * ((7 * series + 1) % size)[None, :]) % size
    angles = 2.0 * np.pi * phase / size
    table = np.zeros((size, TABLE), np.float32)
    table[:, :halves] = np.sin(angles)
    table[:, halves : 2 * halves] = np.cos(angles)
    table[:, 2 * halves] = 1.0
    return table


def inner_kernel(u_hbm, g_hbm, dy_hbm, fi_hbm, ii_hbm, o_hbm, u_ref, g_ref, dy_ref, fi_ref, ii_ref, o_ref, in_sem, out_sem):
    size, channels = u_ref.shape[1:]
    pairs = ROWS // 2
    copies = {}

    def fetch(key, source, target):
        copies[key] = pltpu.make_async_copy(source, target, in_sem.at[len(copies)])
        copies[key].start()

    fetch("fi", fi_hbm, fi_ref)
    for p in range(pairs):
        at = pl.ds(2 * p, 2)
        fetch(("u", p), u_hbm.at[at], u_ref.at[at])
    fetch("ii", ii_hbm, ii_ref)
    for p in range(pairs):
        at = pl.ds(2 * p, 2)
        fetch(("g", p), g_hbm.at[at], g_ref.at[at])
        fetch(("dy", p), dy_hbm.at[at], dy_ref.at[at])

    sends = []

    def emit(which, p, matrix, blocks):
        at = pl.ds(2 * ROWS * p, 2 * ROWS)
        parts = [dot(matrix, block).reshape(PARTS, 1, ROWS, channels) for block in blocks]
        value = jnp.concatenate(parts, 1).reshape(PARTS, 2 * ROWS, channels).astype(BF16)
        o_ref[:, which, 2 * ROWS * p : 2 * ROWS * (p + 1), :] = value
        sends.append(pltpu.make_async_copy(o_ref.at[:, which, at, :], o_hbm.at[:, which, at, :], out_sem.at[len(sends)]))
        sends[-1].start()

    copies["fi"].wait()
    for p in range(pairs):
        copies["u", p].wait()
        emit(0, p, fi_ref[...], [u_ref[2 * p], u_ref[2 * p + 1]])
    copies["ii"].wait()
    turned = ii_ref[...].astype(F32).T.astype(BF16)
    for p in range(pairs):
        copies["g", p].wait()
        copies["dy", p].wait()
        mixed = [
            (g_ref[i].astype(F32) * dy_ref[i].astype(F32)).astype(BF16)
            for i in (2 * p, 2 * p + 1)
        ]
        emit(1, p, turned, mixed)
    for send in sends:
        send.wait()


def filter_kernel(col_ref, tab_ref, fin_ref, bias_ref, hid_ref, hidt_ref, cos_ref, q_ref):
    step = pl.program_id(0)
    size = tab_ref.shape[0]
    hidden = bias_ref.shape[1]
    halves = fin_ref.shape[0] // 2
    col = col_ref[0] + step
    series = lax.broadcasted_iota(jnp.int32, (halves, hidden), 0)
    phase = (((13 * series + 3) % size) * col) % size
    angle = phase.astype(F32) * (2.0 * math.pi / size)
    sq, cq = jnp.sin(angle), jnp.cos(angle)
    q_ref[0, :halves] = cq
    q_ref[0, halves:] = sq
    ws, wc = fin_ref[:halves], fin_ref[halves:]
    weights = jnp.concatenate(
        [
            cq * ws - sq * wc,
            sq * ws + cq * wc,
            bias_ref[...],
            jnp.zeros((TABLE - 2 * halves - 1, hidden), F32),
        ],
        0,
    )
    preact = dot(tab_ref[...], weights, lax.Precision.HIGHEST)
    value = jnp.sin(preact)
    hid_ref[0] = value.astype(BF16)
    hidt_ref[0] = value.T.astype(BF16)
    cos_ref[0] = jnp.cos(preact)


def outer_kernel(r_hbm, *refs):
    sources, (o_hbm, s_ref, x_ref, y_ref, out_ref, wire_ref, spec_ref, tfb_ref, tib_ref), refs = refs[:13], refs[13:22], refs[22:]
    targets, (in_sem, side_sem, out_sem) = refs[:13], refs[13:]
    (fo_ref, tf_ref, w_ref, hid_ref, io_ref, ti_ref, iot_ref, fot_ref, hidt_ref, wt_ref, cos_ref, tabt_ref, q_ref) = targets
    size = fo_ref.shape[0]
    hidden, channels = w_ref.shape
    lanes = x_ref.shape[2]
    halves = q_ref.shape[1] // 2
    rows = wire_ref.shape[2]
    split = channels // lanes
    chunk = PARTS // CHUNKS

    def moved(source, target, sem):
        copies = []
        for which in (0, 1):
            for c in range(CHUNKS):
                at = pl.ds(c * chunk, chunk)
                copies.append(pltpu.make_async_copy(source.at[at, which], target.at[at, which], sem.at[len(copies)]))
        return copies

    loads = moved(r_hbm, wire_ref, in_sem)
    aside = [pltpu.make_async_copy(source, target, side_sem.at[i]) for i, (source, target) in enumerate(zip(sources, targets))]
    for copy in aside[:2] + loads[:CHUNKS] + aside[2:6] + loads[CHUNKS:] + aside[6:]:
        copy.start()
    sends = moved(wire_ref, o_hbm, out_sem)

    def spread(which, ref):
        for c in range(CHUNKS):
            loads[which * CHUNKS + c].wait()
            for part in range(c * chunk, (c + 1) * chunk):
                for i in range(split):
                    ref[i, part * rows : (part + 1) * rows] = wire_ref[part, which, :, i * lanes : (i + 1) * lanes].astype(F32)

    def send(which):
        for c in range(CHUNKS):
            for part in range(c * chunk, (c + 1) * chunk):
                for i in range(split):
                    lane = slice(i * lanes, (i + 1) * lanes)
                    value = [out_ref[i, pl.ds(part * ROWS + a, ROWS, stride=PITCH), :] for a in range(ROWS)]
                    wire_ref[part, which, :, lane] = jnp.concatenate(value, 0).astype(BF16)
            sends[which * CHUNKS + c].start()

    def load(ref, k, scale_ref):
        scale = (tfb_ref if scale_ref is tf_ref else tib_ref)[k]
        mine = pl.ds(k, size, stride=ROWS)
        return jnp.concatenate([(scale * ref[i, mine, :]).astype(BF16) for i in range(split)], 1)

    def store(k, scale_ref, value):
        scale = (tfb_ref if scale_ref is tf_ref else tib_ref)[k]
        for i in range(split):
            out_ref[i, k * PITCH : k * PITCH + size] = scale * value[:, i * lanes : (i + 1) * lanes]

    spread(0, x_ref)
    for copy in aside[:6]:
        copy.wait()
    for k in range(ROWS):
        for narrow, broad in ((tf_ref, tfb_ref), (ti_ref, tib_ref)):
            broad[k] = jnp.broadcast_to(narrow[:, k : k + 1], (size, lanes))
    coming = dot(fo_ref[...], load(x_ref, 0, tf_ref)).astype(BF16)
    for k in range(ROWS):
        spectrum = coming
        spec_ref[k] = spectrum
        if k + 1 < ROWS:
            coming = dot(fo_ref[...], load(x_ref, k + 1, tf_ref)).astype(BF16)
        filtered = (dot(hid_ref[k], w_ref[...]) * spectrum.astype(F32)).astype(BF16)
        store(k, ti_ref, dot(io_ref[...], filtered))
    spread(1, y_ref)
    send(0)
    for copy in aside[6:]:
        copy.wait()

    weight = jnp.zeros((hidden, channels), F32)
    layer = [jnp.zeros((halves, hidden), F32)] * 2
    bias = jnp.zeros((TABLE - 2 * halves, hidden), F32)
    pending = []
    coming = dot(iot_ref[...], load(y_ref, 0, ti_ref))
    for k in range(ROWS):
        grad_filtered = coming
        if k + 1 < ROWS:
            coming = dot(iot_ref[...], load(y_ref, k + 1, ti_ref))
        kernel = dot(hid_ref[k], w_ref[...])
        store(k, tf_ref, dot(fot_ref[...], (grad_filtered * kernel).astype(BF16)))
        grad_kernel = (grad_filtered * spec_ref[k].astype(F32)).astype(BF16)
        weight = weight + dot(hidt_ref[k], grad_kernel)
        pending.append(dot(grad_kernel, wt_ref[...]) * cos_ref[k])
        if len(pending) == 2:
            grad_preact = jnp.concatenate(pending, 1)
            pending = []
            high = grad_preact.astype(BF16)
            low = (grad_preact - high.astype(F32)).astype(BF16)
            upper = dot(tabt_ref[...], high)
            moments = upper[:TABLE] + upper[TABLE:] + dot(tabt_ref[...], low)[:TABLE]
            for i in range(2):
                part = moments[:, i * hidden : (i + 1) * hidden]
                cq, sq = q_ref[k - 1 + i, :halves], q_ref[k - 1 + i, halves:]
                ms, mc = part[:halves], part[halves : 2 * halves]
                layer = [layer[0] + cq * ms + sq * mc, layer[1] + cq * mc - sq * ms]
                bias = bias + part[2 * halves :]
    send(1)

    scale = 1.0 / size
    for i in range(split):
        s_ref[i * hidden : (i + 1) * hidden] = weight[:, i * lanes : (i + 1) * lanes] * scale
    s_ref[split * hidden :] = jnp.concatenate(layer + [bias], 0) * scale
    for copy in sends:
        copy.wait()


def tokens_kernel(x_hbm, dy_ref, ii_ref, fi_ref, gi_hbm, gg_hbm, x_ref, gi_ref, gg_ref, in_sem, out_sem):
    size, channels = dy_ref.shape[1:]
    pairs = ROWS // 2
    loads, sends = {}, []
    for which in (0, 1):
        for p in range(pairs):
            at = pl.ds(2 * ROWS * p, 2 * ROWS)
            loads[which, p] = pltpu.make_async_copy(x_hbm.at[:, which, at, :], x_ref.at[:, which, at, :], in_sem.at[len(loads)])
            loads[which, p].start()

    def operands(which, p):
        loads[which, p].wait()
        value = x_ref[:, which, 2 * ROWS * p : 2 * ROWS * (p + 1), :].astype(F32)
        return [value[:, i * ROWS : (i + 1) * ROWS].reshape(size, channels).astype(BF16) for i in range(2)]

    def emit(source, target, p):
        at = pl.ds(2 * p, 2)
        sends.append(pltpu.make_async_copy(source.at[at], target.at[at], out_sem.at[len(sends)]))
        sends[-1].start()

    for p in range(pairs):
        for i, back in enumerate(operands(0, p)):
            mixed = dot(ii_ref[...], back)
            gg_ref[2 * p + i] = (dy_ref[2 * p + i].astype(F32) * mixed).astype(BF16)
        emit(gg_ref, gg_hbm, p)
    turned = fi_ref[...].astype(F32).T.astype(BF16)
    for p in range(pairs):
        for i, first in enumerate(operands(1, p)):
            gi_ref[2 * p + i] = dot(turned, first).astype(BF16)
        emit(gi_ref, gi_hbm, p)
    for send in sends:
        send.wait()


def finish_kernel(core_ref, mine_ref, other_ref, w_ref, l_ref, b_ref):
    hidden = w_ref.shape[0]
    features = l_ref.shape[0]
    half, lanes = mine_ref.shape
    mine, other = mine_ref[...], other_ref[...]
    lower = jnp.where(core_ref[0] == 0, mine, other)
    upper = jnp.where(core_ref[0] == 0, other, mine)
    w_ref[:, :lanes] = lower[:hidden]
    w_ref[: half - hidden, lanes:] = lower[hidden:]
    w_ref[half - hidden :, lanes:] = upper[: 2 * hidden - half]
    l_ref[...] = upper[2 * hidden - half : 2 * hidden - half + features]
    b_ref[...] = upper[2 * hidden - half + features : 2 * hidden - half + features + 1]


def after(value, *others):
    return lax.optimization_barrier((value,) + others)[0]


def params(limit, axes=1):
    return pltpu.CompilerParams(
        vmem_limit_bytes=limit * MIB, dimension_semantics=("arbitrary",) * axes
    )


def exchanged(value, axis, count, step):
    return lax.ppermute(value, axis, [(i, i ^ step) for i in range(count)])


def doubled(value, axis, count, steps):
    for step in steps:
        value = value + exchanged(value, axis, count, step)
    return value


def shards(
    gated_input,
    out_gate,
    grad_out,
    forward_inner,
    forward_outer,
    inverse_outer,
    inverse_inner,
    twiddle_forward,
    twiddle_inverse,
    filter_in,
    filter_bias,
    filter_out,
):
    size = forward_outer.shape[0]
    channels = gated_input.shape[1]
    hidden = filter_in.shape[1]
    features = filter_in.shape[0]
    lanes = 128
    tokens = (ROWS, size, channels)
    inputs, gates, upstream = (x.reshape(tokens) for x in (gated_input, out_gate, grad_out))
    square = (size, size)
    pair = pl.BlockSpec((2, size, channels), lambda p: (p, 0, 0))
    wire = (PARTS, 2, ROWS * ROWS, channels)
    wire_pair = pl.BlockSpec((PARTS, 2, 2 * ROWS, channels), lambda p: (0, 0, p, 0))

    anywhere = pl.BlockSpec(memory_space=pltpu.HBM)
    inside = pl.BlockSpec(memory_space=pltpu.VMEM)
    sent = pl.pallas_call(
        inner_kernel,
        out_shape=jax.ShapeDtypeStruct(wire, BF16),
        in_specs=[anywhere] * 5,
        out_specs=anywhere,
        scratch_shapes=[pltpu.VMEM(tokens, BF16)] * 3
        + [pltpu.VMEM(square, BF16)] * 2
        + [pltpu.VMEM(wire, BF16), pltpu.SemaphoreType.DMA((2 + 3 * ROWS // 2,)), pltpu.SemaphoreType.DMA((ROWS,))],
        compiler_params=pltpu.CompilerParams(vmem_limit_bytes=62 * MIB),
        cost_estimate=pl.CostEstimate(flops=4 * ROWS * size * size * channels, bytes_accessed=10 * MIB, transcendentals=0),
        name="inner_transforms",
    )(inputs, gates, upstream, forward_inner, inverse_inner)

    column = lax.axis_index("seq").astype(jnp.int32).reshape(1) * ROWS
    sent, column = lax.optimization_barrier((sent, column))
    received = lax.all_to_all(sent, "seq", split_axis=0, concat_axis=0, tiled=True)

    table = outer_table(size, features // 2)
    each = lambda *shape: pl.BlockSpec((1,) + shape, lambda k, *_: (k,) + (0,) * len(shape))
    made = [
        ((size, hidden), BF16),
        ((hidden, size), BF16),
        ((size, hidden), F32),
        ((features, hidden), F32),
    ]
    generated = pl.pallas_call(
        filter_kernel,
        grid_spec=pltpu.PrefetchScalarGridSpec(
            num_scalar_prefetch=1,
            grid=(ROWS,),
            in_specs=[full((size, TABLE)), full((features, hidden)), full((1, hidden))],
            out_specs=[each(*shape) for shape, _ in made],
        ),
        out_shape=[jax.ShapeDtypeStruct((ROWS,) + shape, kind) for shape, kind in made],
        compiler_params=params(32),
        cost_estimate=pl.CostEstimate(flops=40 * MIB, bytes_accessed=9 * MIB, transcendentals=2 * MIB),
        name="filter_generator",
    )(column, table, filter_in, filter_bias.reshape(1, hidden))

    small = (2 * hidden + TABLE, lanes)
    high = table.T.astype(BF16)
    low = (table.T - high.astype(np.float32)).astype(BF16)
    hid, hidt, cosine, turns = generated
    aside = [
        forward_outer, twiddle_forward, filter_out, hid, inverse_outer, twiddle_inverse,
        inverse_outer.T, forward_outer.T, hidt, filter_out.T, cosine, np.concatenate([high, low], 0), turns,
    ]
    returned, partial = pl.pallas_call(
        outer_kernel,
        out_shape=[jax.ShapeDtypeStruct(wire, BF16), jax.ShapeDtypeStruct(small, F32)],
        in_specs=[anywhere] * 14,
        out_specs=[anywhere, inside],
        scratch_shapes=[pltpu.VMEM((channels // lanes, ROWS * size, lanes), F32)] * 2
        + [pltpu.VMEM((channels // lanes, ROWS * PITCH, lanes), F32)]
        + [pltpu.VMEM(wire, BF16), pltpu.VMEM(tokens, BF16)]
        + [pltpu.VMEM((ROWS, size, lanes), F32)] * 2
        + [pltpu.VMEM(array.shape, array.dtype) for array in aside]
        + [pltpu.SemaphoreType.DMA((count,)) for count in (2 * CHUNKS, len(aside), 2 * CHUNKS)],
        compiler_params=pltpu.CompilerParams(vmem_limit_bytes=OUTER_LIMIT * MIB),
        cost_estimate=pl.CostEstimate(flops=10 * ROWS * size * size * channels, bytes_accessed=18 * MIB, transcendentals=0),
        name="outer_transforms",
    )(received, *aside)

    arrived = lax.all_to_all(returned, "seq", split_axis=0, concat_axis=0, tiled=True)

    layer = doubled(partial[2 * hidden :], "ch", 4, (1, 2))
    total = jnp.concatenate([partial[: 2 * hidden], layer], 0)
    half = small[0] // 2
    lower, upper = total[:half], total[half:]
    core = lax.axis_index("seq") % 2
    mine = jnp.where(core == 0, lower, upper)
    mine = mine + exchanged(jnp.where(core == 0, upper, lower), "seq", PARTS, 1)
    mine = doubled(mine, "seq", PARTS, (16, 32, 8))
    other = exchanged(mine, "seq", PARTS, 4)

    grad_input, grad_gate = pl.pallas_call(
        tokens_kernel,
        out_shape=[jax.ShapeDtypeStruct(tokens, BF16)] * 2,
        in_specs=[anywhere, inside, inside, inside],
        out_specs=[anywhere] * 2,
        scratch_shapes=[pltpu.VMEM(wire, BF16), pltpu.VMEM(tokens, BF16), pltpu.VMEM(tokens, BF16), pltpu.SemaphoreType.DMA((ROWS,)), pltpu.SemaphoreType.DMA((ROWS,))],
        compiler_params=pltpu.CompilerParams(vmem_limit_bytes=32 * MIB),
        cost_estimate=pl.CostEstimate(flops=4 * ROWS * size * size * channels, bytes_accessed=10 * MIB, transcendentals=0),
        name="token_gradients",
    )(arrived, upstream, inverse_inner, forward_inner)
    mine = doubled(mine + after(other, grad_gate), "seq", PARTS, (2,))
    weight_grad, layer_grad, bias_grad = pl.pallas_call(
        finish_kernel,
        out_shape=[
            jax.ShapeDtypeStruct((hidden, channels), F32),
            jax.ShapeDtypeStruct((features, hidden), F32),
            jax.ShapeDtypeStruct((1, hidden), F32),
        ],
        in_specs=[pl.BlockSpec(memory_space=pltpu.SMEM), inside, inside],
        name="weight_gradients",
    )(core.astype(jnp.int32).reshape(1), mine, exchanged(mine, "seq", PARTS, 1))
    flat = (ROWS * size, channels)
    return grad_input.reshape(flat), grad_gate.reshape(flat), weight_grad, layer_grad, bias_grad.reshape(hidden)


def solution(mesh):
    return jax.shard_map(
        shards,
        mesh=mesh,
        in_specs=(
            P("seq", "ch"),
            P("seq", "ch"),
            P("seq", "ch"),
            P(),
            P(),
            P(),
            P(),
            P(None, "seq"),
            P(None, "seq"),
            P(),
            P(),
            P(None, "ch"),
        ),
        out_specs=(P("seq", "ch"), P("seq", "ch"), P(None, "ch"), P(), P()),
        check_vma=False,
    )
```

```python
import functools
import math

import jax
import jax.numpy as jnp
import numpy as np
from jax import lax
from jax.experimental import pallas as pl
from jax.experimental.pallas import tpu as pltpu
from jax.sharding import PartitionSpec as P

F32 = jnp.float32
BF16 = jnp.bfloat16
MIB = 1 << 20
PARTS = 64
ROWS = 8
OUTER_LIMIT = 62
CHUNKS = 8
PITCH = 521
TABLE = 48


def dot(x, y, precision=None):
    return lax.dot_general(
        x, y, (((1,), (0,)), ((), ())), precision=precision, preferred_element_type=F32
    )


def full(shape, buffers=1):
    return pl.BlockSpec(
        shape, lambda *_: (0,) * len(shape), pipeline_mode=pl.Buffered(buffers)
    )


def outer_table(size, halves):
    series = np.arange(halves)
    phase = (np.arange(size)[:, None] * ((7 * series + 1) % size)[None, :]) % size
    angles = 2.0 * np.pi * phase / size
    table = np.zeros((size, TABLE), np.float32)
    table[:, :halves] = np.sin(angles)
    table[:, halves : 2 * halves] = np.cos(angles)
    table[:, 2 * halves] = 1.0
    return table


def inner_kernel(u_hbm, g_hbm, dy_hbm, fi_hbm, ii_hbm, o_hbm, u_ref, g_ref, dy_ref, fi_ref, ii_ref, o_ref, in_sem, out_sem):
    size, channels = u_ref.shape[1:]
    pairs = ROWS // 2
    copies = {}

    def fetch(key, source, target):
        copies[key] = pltpu.make_async_copy(source, target, in_sem.at[len(copies)])
        copies[key].start()

    fetch("fi", fi_hbm, fi_ref)
    for p in range(pairs):
        at = pl.ds(2 * p, 2)
        fetch(("u", p), u_hbm.at[at], u_ref.at[at])
    fetch("ii", ii_hbm, ii_ref)
    for p in range(pairs):
        at = pl.ds(2 * p, 2)
        fetch(("g", p), g_hbm.at[at], g_ref.at[at])
        fetch(("dy", p), dy_hbm.at[at], dy_ref.at[at])

    sends = []

    def emit(which, p, matrix, blocks):
        at = pl.ds(2 * ROWS * p, 2 * ROWS)
        parts = [dot(matrix, block).reshape(PARTS, 1, ROWS, channels) for block in blocks]
        value = jnp.concatenate(parts, 1).reshape(PARTS, 2 * ROWS, channels).astype(BF16)
        o_ref[:, which, 2 * ROWS * p : 2 * ROWS * (p + 1), :] = value
        sends.append(pltpu.make_async_copy(o_ref.at[:, which, at, :], o_hbm.at[:, which, at, :], out_sem.at[len(sends)]))
        sends[-1].start()

    copies["fi"].wait()
    for p in range(pairs):
        copies["u", p].wait()
        emit(0, p, fi_ref[...], [u_ref[2 * p], u_ref[2 * p + 1]])
    copies["ii"].wait()
    turned = ii_ref[...].astype(F32).T.astype(BF16)
    for p in range(pairs):
        copies["g", p].wait()
        copies["dy", p].wait()
        mixed = [
            (g_ref[i].astype(F32) * dy_ref[i].astype(F32)).astype(BF16)
            for i in (2 * p, 2 * p + 1)
        ]
        emit(1, p, turned, mixed)
    for send in sends:
        send.wait()


def filter_kernel(col_ref, tab_ref, fin_ref, bias_ref, hid_ref, hidt_ref, cos_ref, q_ref):
    step = pl.program_id(0)
    size = tab_ref.shape[0]
    hidden = bias_ref.shape[1]
    halves = fin_ref.shape[0] // 2
    col = col_ref[0] + step
    series = lax.broadcasted_iota(jnp.int32, (halves, hidden), 0)
    phase = (((13 * series + 3) % size) * col) % size
    angle = phase.astype(F32) * (2.0 * math.pi / size)
    sq, cq = jnp.sin(angle), jnp.cos(angle)
    q_ref[0, :halves] = cq
    q_ref[0, halves:] = sq
    ws, wc = fin_ref[:halves], fin_ref[halves:]
    weights = jnp.concatenate(
        [
            cq * ws - sq * wc,
            sq * ws + cq * wc,
            bias_ref[...],
            jnp.zeros((TABLE - 2 * halves - 1, hidden), F32),
        ],
        0,
    )
    preact = dot(tab_ref[...], weights, lax.Precision.HIGHEST)
    value = jnp.sin(preact)
    hid_ref[0] = value.astype(BF16)
    hidt_ref[0] = value.T.astype(BF16)
    cos_ref[0] = jnp.cos(preact)


def outer_kernel(r_hbm, *refs):
    sources, (o_hbm, s_ref, x_ref, y_ref, out_ref, wire_ref, spec_ref, tfb_ref, tib_ref), refs = refs[:13], refs[13:22], refs[22:]
    targets, (in_sem, side_sem, out_sem) = refs[:13], refs[13:]
    (fo_ref, tf_ref, w_ref, hid_ref, io_ref, ti_ref, iot_ref, fot_ref, hidt_ref, wt_ref, cos_ref, tabt_ref, q_ref) = targets
    size = fo_ref.shape[0]
    hidden, channels = w_ref.shape
    lanes = x_ref.shape[2]
    halves = q_ref.shape[1] // 2
    rows = wire_ref.shape[2]
    split = channels // lanes
    chunk = PARTS // CHUNKS

    def moved(source, target, sem):
        copies = []
        for which in (0, 1):
            for c in range(CHUNKS):
                at = pl.ds(c * chunk, chunk)
                copies.append(pltpu.make_async_copy(source.at[at, which], target.at[at, which], sem.at[len(copies)]))
        return copies

    loads = moved(r_hbm, wire_ref, in_sem)
    aside = [pltpu.make_async_copy(source, target, side_sem.at[i]) for i, (source, target) in enumerate(zip(sources, targets))]
    for copy in aside[:2] + loads[:CHUNKS] + aside[2:6] + loads[CHUNKS:] + aside[6:]:
        copy.start()
    sends = moved(wire_ref, o_hbm, out_sem)

    def spread(which, ref):
        for c in range(CHUNKS):
            loads[which * CHUNKS + c].wait()
            for part in range(c * chunk, (c + 1) * chunk):
                for i in range(split):
                    ref[i, part * rows : (part + 1) * rows] = wire_ref[part, which, :, i * lanes : (i + 1) * lanes].astype(F32)

    def send(which):
        for c in range(CHUNKS):
            for part in range(c * chunk, (c + 1) * chunk):
                for i in range(split):
                    lane = slice(i * lanes, (i + 1) * lanes)
                    value = [out_ref[i, pl.ds(part * ROWS + a, ROWS, stride=PITCH), :] for a in range(ROWS)]
                    wire_ref[part, which, :, lane] = jnp.concatenate(value, 0).astype(BF16)
            sends[which * CHUNKS + c].start()

    def load(ref, k, scale_ref):
        scale = (tfb_ref if scale_ref is tf_ref else tib_ref)[k]
        mine = pl.ds(k, size, stride=ROWS)
        return jnp.concatenate([(scale * ref[i, mine, :]).astype(BF16) for i in range(split)], 1)

    def store(k, scale_ref, value):
        scale = (tfb_ref if scale_ref is tf_ref else tib_ref)[k]
        for i in range(split):
            out_ref[i, k * PITCH : k * PITCH + size] = scale * value[:, i * lanes : (i + 1) * lanes]

    spread(0, x_ref)
    for copy in aside[:6]:
        copy.wait()
    for k in range(ROWS):
        for narrow, broad in ((tf_ref, tfb_ref), (ti_ref, tib_ref)):
            broad[k] = jnp.broadcast_to(narrow[:, k : k + 1], (size, lanes))
    coming = dot(fo_ref[...], load(x_ref, 0, tf_ref)).astype(BF16)
    for k in range(ROWS):
        spectrum = coming
        spec_ref[k] = spectrum
        if k + 1 < ROWS:
            coming = dot(fo_ref[...], load(x_ref, k + 1, tf_ref)).astype(BF16)
        filtered = (dot(hid_ref[k], w_ref[...]) * spectrum.astype(F32)).astype(BF16)
        store(k, ti_ref, dot(io_ref[...], filtered))
    spread(1, y_ref)
    send(0)
    for copy in aside[6:8]:
        copy.wait()

    weight = jnp.zeros((hidden, channels), F32)
    layer = [jnp.zeros((halves, hidden), F32)] * 2
    bias = jnp.zeros((TABLE - 2 * halves, hidden), F32)
    pending = []
    coming = dot(iot_ref[...], load(y_ref, 0, ti_ref))
    for copy in aside[8:]:
        copy.wait()
    for k in range(ROWS):
        grad_filtered = coming
        if k + 1 < ROWS:
            coming = dot(iot_ref[...], load(y_ref, k + 1, ti_ref))
        kernel = dot(hid_ref[k], w_ref[...])
        store(k, tf_ref, dot(fot_ref[...], (grad_filtered * kernel).astype(BF16)))
        grad_kernel = (grad_filtered * spec_ref[k].astype(F32)).astype(BF16)
        weight = weight + dot(hidt_ref[k], grad_kernel)
        pending.append(dot(grad_kernel, wt_ref[...]) * cos_ref[k])
        if len(pending) == 2:
            grad_preact = jnp.concatenate(pending, 1)
            pending = []
            high = grad_preact.astype(BF16)
            low = (grad_preact - high.astype(F32)).astype(BF16)
            upper = dot(tabt_ref[...], high)
            moments = upper[:TABLE] + upper[TABLE:] + dot(tabt_ref[...], low)[:TABLE]
            for i in range(2):
                part = moments[:, i * hidden : (i + 1) * hidden]
                cq, sq = q_ref[k - 1 + i, :halves], q_ref[k - 1 + i, halves:]
                ms, mc = part[:halves], part[halves : 2 * halves]
                layer = [layer[0] + cq * ms + sq * mc, layer[1] + cq * mc - sq * ms]
                bias = bias + part[2 * halves :]
    send(1)

    scale = 1.0 / size
    for i in range(split):
        s_ref[i * hidden : (i + 1) * hidden] = weight[:, i * lanes : (i + 1) * lanes] * scale
    s_ref[split * hidden :] = jnp.concatenate(layer + [bias], 0) * scale
    for copy in sends:
        copy.wait()


def tokens_kernel(x_hbm, dy_ref, ii_ref, fi_ref, gi_hbm, gg_hbm, x_ref, gi_ref, gg_ref, in_sem, out_sem):
    size, channels = dy_ref.shape[1:]
    pairs = ROWS // 2
    loads, sends = {}, []
    for which in (0, 1):
        for p in range(pairs):
            at = pl.ds(2 * ROWS * p, 2 * ROWS)
            loads[which, p] = pltpu.make_async_copy(x_hbm.at[:, which, at, :], x_ref.at[:, which, at, :], in_sem.at[len(loads)])
            loads[which, p].start()

    def operands(which, p):
        loads[which, p].wait()
        value = x_ref[:, which, 2 * ROWS * p : 2 * ROWS * (p + 1), :].astype(F32)
        return [value[:, i * ROWS : (i + 1) * ROWS].reshape(size, channels).astype(BF16) for i in range(2)]

    def emit(source, target, p):
        at = pl.ds(2 * p, 2)
        sends.append(pltpu.make_async_copy(source.at[at], target.at[at], out_sem.at[len(sends)]))
        sends[-1].start()

    for p in range(pairs):
        for i, back in enumerate(operands(0, p)):
            mixed = dot(ii_ref[...], back)
            gg_ref[2 * p + i] = (dy_ref[2 * p + i].astype(F32) * mixed).astype(BF16)
        emit(gg_ref, gg_hbm, p)
    turned = fi_ref[...].astype(F32).T.astype(BF16)
    for p in range(pairs):
        for i, first in enumerate(operands(1, p)):
            gi_ref[2 * p + i] = dot(turned, first).astype(BF16)
        emit(gi_ref, gi_hbm, p)
    for send in sends:
        send.wait()


def finish_kernel(core_ref, mine_ref, other_ref, w_ref, l_ref, b_ref):
    hidden = w_ref.shape[0]
    features = l_ref.shape[0]
    half, lanes = mine_ref.shape
    mine, other = mine_ref[...], other_ref[...]
    lower = jnp.where(core_ref[0] == 0, mine, other)
    upper = jnp.where(core_ref[0] == 0, other, mine)
    w_ref[:, :lanes] = lower[:hidden]
    w_ref[: half - hidden, lanes:] = lower[hidden:]
    w_ref[half - hidden :, lanes:] = upper[: 2 * hidden - half]
    l_ref[...] = upper[2 * hidden - half : 2 * hidden - half + features]
    b_ref[...] = upper[2 * hidden - half + features : 2 * hidden - half + features + 1]


def after(value, *others):
    return lax.optimization_barrier((value,) + others)[0]


def params(limit, axes=1):
    return pltpu.CompilerParams(
        vmem_limit_bytes=limit * MIB, dimension_semantics=("arbitrary",) * axes
    )


def exchanged(value, axis, count, step):
    return lax.ppermute(value, axis, [(i, i ^ step) for i in range(count)])


def doubled(value, axis, count, steps):
    for step in steps:
        value = value + exchanged(value, axis, count, step)
    return value


def shards(
    gated_input,
    out_gate,
    grad_out,
    forward_inner,
    forward_outer,
    inverse_outer,
    inverse_inner,
    twiddle_forward,
    twiddle_inverse,
    filter_in,
    filter_bias,
    filter_out,
):
    size = forward_outer.shape[0]
    channels = gated_input.shape[1]
    hidden = filter_in.shape[1]
    features = filter_in.shape[0]
    lanes = 128
    tokens = (ROWS, size, channels)
    inputs, gates, upstream = (x.reshape(tokens) for x in (gated_input, out_gate, grad_out))
    square = (size, size)
    pair = pl.BlockSpec((2, size, channels), lambda p: (p, 0, 0))
    wire = (PARTS, 2, ROWS * ROWS, channels)
    wire_pair = pl.BlockSpec((PARTS, 2, 2 * ROWS, channels), lambda p: (0, 0, p, 0))

    anywhere = pl.BlockSpec(memory_space=pltpu.HBM)
    inside = pl.BlockSpec(memory_space=pltpu.VMEM)
    sent = pl.pallas_call(
        inner_kernel,
        out_shape=jax.ShapeDtypeStruct(wire, BF16),
        in_specs=[anywhere] * 5,
        out_specs=anywhere,
        scratch_shapes=[pltpu.VMEM(tokens, BF16)] * 3
        + [pltpu.VMEM(square, BF16)] * 2
        + [pltpu.VMEM(wire, BF16), pltpu.SemaphoreType.DMA((2 + 3 * ROWS // 2,)), pltpu.SemaphoreType.DMA((ROWS,))],
        compiler_params=pltpu.CompilerParams(vmem_limit_bytes=62 * MIB),
        cost_estimate=pl.CostEstimate(flops=4 * ROWS * size * size * channels, bytes_accessed=10 * MIB, transcendentals=0),
        name="inner_transforms",
    )(inputs, gates, upstream, forward_inner, inverse_inner)

    column = lax.axis_index("seq").astype(jnp.int32).reshape(1) * ROWS
    sent, column = lax.optimization_barrier((sent, column))
    received = lax.all_to_all(sent, "seq", split_axis=0, concat_axis=0, tiled=True)

    table = outer_table(size, features // 2)
    each = lambda *shape: pl.BlockSpec((1,) + shape, lambda k, *_: (k,) + (0,) * len(shape))
    made = [
        ((size, hidden), BF16),
        ((hidden, size), BF16),
        ((size, hidden), F32),
        ((features, hidden), F32),
    ]
    generated = pl.pallas_call(
        filter_kernel,
        grid_spec=pltpu.PrefetchScalarGridSpec(
            num_scalar_prefetch=1,
            grid=(ROWS,),
            in_specs=[full((size, TABLE)), full((features, hidden)), full((1, hidden))],
            out_specs=[each(*shape) for shape, _ in made],
        ),
        out_shape=[jax.ShapeDtypeStruct((ROWS,) + shape, kind) for shape, kind in made],
        compiler_params=params(32),
        cost_estimate=pl.CostEstimate(flops=40 * MIB, bytes_accessed=9 * MIB, transcendentals=2 * MIB),
        name="filter_generator",
    )(column, table, filter_in, filter_bias.reshape(1, hidden))

    small = (2 * hidden + TABLE, lanes)
    high = table.T.astype(BF16)
    low = (table.T - high.astype(np.float32)).astype(BF16)
    hid, hidt, cosine, turns = generated
    aside = [
        forward_outer, twiddle_forward, filter_out, hid, inverse_outer, twiddle_inverse,
        inverse_outer.T, forward_outer.T, hidt, filter_out.T, cosine, np.concatenate([high, low], 0), turns,
    ]
    returned, partial = pl.pallas_call(
        outer_kernel,
        out_shape=[jax.ShapeDtypeStruct(wire, BF16), jax.ShapeDtypeStruct(small, F32)],
        in_specs=[anywhere] * 14,
        out_specs=[anywhere, inside],
        scratch_shapes=[pltpu.VMEM((channels // lanes, ROWS * size, lanes), F32)] * 2
        + [pltpu.VMEM((channels // lanes, ROWS * PITCH, lanes), F32)]
        + [pltpu.VMEM(wire, BF16), pltpu.VMEM(tokens, BF16)]
        + [pltpu.VMEM((ROWS, size, lanes), F32)] * 2
        + [pltpu.VMEM(array.shape, array.dtype) for array in aside]
        + [pltpu.SemaphoreType.DMA((count,)) for count in (2 * CHUNKS, len(aside), 2 * CHUNKS)],
        compiler_params=pltpu.CompilerParams(vmem_limit_bytes=OUTER_LIMIT * MIB),
        cost_estimate=pl.CostEstimate(flops=10 * ROWS * size * size * channels, bytes_accessed=18 * MIB, transcendentals=0),
        name="outer_transforms",
    )(received, *aside)

    arrived = lax.all_to_all(returned, "seq", split_axis=0, concat_axis=0, tiled=True)

    layer = doubled(partial[2 * hidden :], "ch", 4, (1, 2))
    total = jnp.concatenate([partial[: 2 * hidden], layer], 0)
    half = small[0] // 2
    lower, upper = total[:half], total[half:]
    core = lax.axis_index("seq") % 2
    mine = jnp.where(core == 0, lower, upper)
    mine = mine + exchanged(jnp.where(core == 0, upper, lower), "seq", PARTS, 1)
    mine = doubled(mine, "seq", PARTS, (16, 32, 8))
    other = exchanged(mine, "seq", PARTS, 4)

    grad_input, grad_gate = pl.pallas_call(
        tokens_kernel,
        out_shape=[jax.ShapeDtypeStruct(tokens, BF16)] * 2,
        in_specs=[anywhere, inside, inside, inside],
        out_specs=[anywhere] * 2,
        scratch_shapes=[pltpu.VMEM(wire, BF16), pltpu.VMEM(tokens, BF16), pltpu.VMEM(tokens, BF16), pltpu.SemaphoreType.DMA((ROWS,)), pltpu.SemaphoreType.DMA((ROWS,))],
        compiler_params=pltpu.CompilerParams(vmem_limit_bytes=32 * MIB),
        cost_estimate=pl.CostEstimate(flops=4 * ROWS * size * size * channels, bytes_accessed=10 * MIB, transcendentals=0),
        name="token_gradients",
    )(arrived, upstream, inverse_inner, forward_inner)
    mine = doubled(mine + after(other, grad_gate), "seq", PARTS, (2,))
    weight_grad, layer_grad, bias_grad = pl.pallas_call(
        finish_kernel,
        out_shape=[
            jax.ShapeDtypeStruct((hidden, channels), F32),
            jax.ShapeDtypeStruct((features, hidden), F32),
            jax.ShapeDtypeStruct((1, hidden), F32),
        ],
        in_specs=[pl.BlockSpec(memory_space=pltpu.SMEM), inside, inside],
        name="weight_gradients",
    )(core.astype(jnp.int32).reshape(1), mine, exchanged(mine, "seq", PARTS, 1))
    flat = (ROWS * size, channels)
    return grad_input.reshape(flat), grad_gate.reshape(flat), weight_grad, layer_grad, bias_grad.reshape(hidden)


def solution(mesh):
    return jax.shard_map(
        shards,
        mesh=mesh,
        in_specs=(
            P("seq", "ch"),
            P("seq", "ch"),
            P("seq", "ch"),
            P(),
            P(),
            P(),
            P(),
            P(None, "seq"),
            P(None, "seq"),
            P(),
            P(),
            P(None, "ch"),
        ),
        out_specs=(P("seq", "ch"), P("seq", "ch"), P(None, "ch"), P(), P()),
        check_vma=False,
    )
```
